32 devices in a mesh: grp: 2 (over x), row: 8 (over z, y), col: 2 (over core).
Axes of the slice: x: 2, y: 2, z: 4, core: 2. Of those that a mesh axis runs over, the one named last changes fastest.
Arguments:
- counts: bfloat16 [256, 256, 256], P(('grp', 'row', 'col')), parts along dimension 0, may hold values from 1 to 576, as said below
- tile_pos: int32 [256], P(('grp', 'row', 'col')), parts along dimension 0, may hold values from -1 to 7, as said below
- omega_t: bfloat16 [64, 32768], P(None, 'col'), may hold values from -0.09375 to 0.09375
- psi: bfloat16 [64, 2048], P(None, 'row'), may hold values from -0.125 to 0.125
Outputs:
- range_sketch: float32 [64, 4096], P(None, ('grp', 'row')), parts along dimension 1
- corange: float32 [64, 65536], P(None, ('grp', 'col', 'row')), parts along dimension 1
The draws below stay inside these ranges and needn't reach their ends.
There are 2 independent parts, one for each index of `grp`. The reference program is written for one: setup_inputs(seed, part) draws one part's arguments, and reference() takes and returns one part's arrays. A program takes and returns all parts, laid end to end along the dimension named above; an argument that names none is the same for every part. Nothing has to cross between parts.
Inputs may be any that keep to these rules, and one draw needn't show every extreme that they name: Positive counts; entries of empty slots are ignored. `tile_pos`: slot d of every device refers to a block of the d-th column range; every device holds at least one tile; in every draw some device fills all 8 slots and some column range receives a tile from every device of a col index.
All inputs are finite; a program needn't handle non-finite values.
Results may differ from the reference program's by a relative error of at most 0.003.
Values sent between devices are 32-bit elements; how exact they have to be, the bound alone decides.
No kernel may reach another device: no remote copies, remote signals or barrier semaphores. Data moves between devices by JAX's collectives and lax.ppermute only.
A program may use at most 128 MiB of HBM per device.

```python
import math
import jax
import jax.numpy as jnp
from jax import lax

TILE = 256
RANK = 64
BPO = 8
ITEMS = 2048
CONTEXTS = 32768
N_ROW = 8
N_COL = 2


def draw_tile_pos(key, part):
    key = jax.random.fold_in(key, 1)
    keys = jax.random.split(key, 5)
    shape = (N_ROW, N_COL, N_ROW)
    expo = jax.random.randint(keys[0], (N_ROW, N_COL, 1), 0, 4)
    level = jnp.array([1, 2, 4, 8], dtype=jnp.int32)[expo]
    coin = jax.random.randint(keys[1], shape, 0, 8)
    live = coin < level
    full_row = jax.random.randint(keys[2], (1, N_COL, 1), 0, N_ROW)
    full_owner = jax.random.randint(keys[3], (1, N_COL, 1), 0, N_ROW)
    row_ids = jnp.arange(N_ROW, dtype=jnp.int32).reshape(N_ROW, 1, 1)
    slot_ids = jnp.arange(N_ROW, dtype=jnp.int32).reshape(1, 1, N_ROW)
    live = live | (row_ids == full_row) | (slot_ids == full_owner)
    empty_row = (full_row + 1) % N_ROW
    empty_slot = (full_owner + 1) % N_ROW
    live = live & jnp.logical_not((row_ids == empty_row) & (slot_ids == empty_slot))
    where_pos = jax.random.randint(keys[4], shape, 0, BPO)
    where_pos = jnp.where((row_ids == full_row) & (slot_ids == full_owner), BPO - 1, where_pos)
    return jnp.where(live, where_pos, -1).reshape(-1).astype(jnp.int32)


def draw_counts(key, part):
    key = jax.random.fold_in(key, 2)
    keys = jax.random.split(key, 2)
    shape = (N_ROW, N_COL, N_ROW, TILE, TILE)
    rise = 1.0 + 2.0 * jnp.arange(N_ROW, dtype=jnp.float32).reshape(N_ROW, 1, 1, 1, 1) / (N_ROW - 1)
    item = jnp.exp(jax.random.uniform(keys[0], (N_ROW, 1, 1, TILE, 1), jnp.float32, 0.0, math.log(3.0)))
    base = jnp.exp(jax.random.uniform(keys[1], shape, jnp.float32, 0.0, math.log(16.0)))
    return (base * item * rise).reshape(N_ROW * N_COL * N_ROW, TILE, TILE).astype(jnp.bfloat16)


def shard_levels(rng, shape, pieces, low, high):
    def one(dim, shards_of):
        steps = jax.random.uniform(jax.random.fold_in(jax.random.fold_in(rng, 6), dim), (shards_of,), jnp.float32, low / len(pieces), high / len(pieces))
        return jnp.repeat(jnp.exp(steps), shape[dim] // shards_of).reshape((-1,) + (1,) * (len(shape) - dim - 1))

    factor_of = one(*pieces[0])
    for cut in pieces[1:]:
        factor_of = factor_of * one(*cut)
    return factor_of


def gaussian(key, extent, scale, reach, cuts=(), kind=jnp.bfloat16):
    entries = scale * jax.random.normal(key, extent, jnp.float32)
    if cuts:
        entries = entries * shard_levels(key, extent, cuts, -0.22, 0.18)
    return jnp.clip(entries, -reach, reach).astype(kind)


def setup_inputs(seed: int = 0, part: int = 0) -> dict:
    streams_of = jax.random.split(jax.random.key(seed), 5)
    part_keys = jax.random.split(jax.random.fold_in(streams_of[4], part), 5)
    counts = draw_counts(jax.random.fold_in(jax.random.fold_in(streams_of[4], part), 71), part)
    tile_pos = draw_tile_pos(jax.random.fold_in(jax.random.fold_in(streams_of[4], part), 71), part)
    omega_t = gaussian(streams_of[2], (RANK, CONTEXTS), (TILE * N_ROW * N_COL) ** -0.5, 0.09375, ((1, 2),))
    psi = gaussian(streams_of[3], (RANK, ITEMS), (TILE * N_ROW) ** -0.5, 0.125, ((1, 8),))
    return dict(counts=counts, tile_pos=tile_pos, omega_t=omega_t, psi=psi)


shift_log = math.log(5.0)
highest = lax.Precision.HIGHEST


def reference(counts, tile_pos, omega_t, psi):
    rank = omega_t.shape[0]
    live = (tile_pos >= 0).reshape(N_ROW, N_COL, N_ROW)
    position = tile_pos.reshape(N_ROW, N_COL, N_ROW)
    select = (position[..., None] == jnp.arange(BPO, dtype=jnp.int32)).astype(jnp.float32)
    tiles = counts.reshape(N_ROW, N_COL, N_ROW, TILE, TILE)

    def sums(args):
        block, alive = args
        values = jnp.where(alive[:, :, None, None], block.astype(jnp.float32), 0.0)
        return jnp.sum(values, axis=(0, 1, 3)), jnp.sum(values, axis=2)

    row_sums, column_parts = lax.map(sums, (tiles, live))
    column_sums = jnp.einsum("acdb,acdt->cdbt", select, column_parts, precision=highest)
    smoothing_power = column_sums ** 0.75
    total = jnp.sum(smoothing_power)
    omega_five = omega_t.astype(jnp.float32).reshape(rank, N_COL, N_ROW, BPO, TILE)
    corange_test_blocks = psi.astype(jnp.float32).reshape(rank, N_ROW, TILE).transpose(1, 0, 2)

    def one_row(carry, args):
        block, alive, chosen, rows, psi_rows = args
        smooth_tile = jnp.einsum("cdb,cdbt->cdt", chosen, smoothing_power, precision=highest)
        safe = jnp.where(alive[..., None], smooth_tile, 1.0)
        safe_counts = jnp.where(alive[..., None, None], block.astype(jnp.float32), 1.0)
        pmi = jnp.log(safe_counts) + (jnp.log(total) - jnp.log(rows))[None, None, :, None] - jnp.log(safe)[:, :, None, :]
        shifted_pmi_matrix = jnp.where(alive[..., None, None], jnp.maximum(pmi - shift_log, 0.0), 0.0).astype(jnp.bfloat16).astype(jnp.float32)
        selected_test_rows = jnp.einsum("cdb,rcdbt->rcdt", chosen, omega_five, precision=highest)
        range_rows = jnp.einsum("rcdt,cdit->ri", selected_test_rows, shifted_pmi_matrix, precision=highest)
        partial_contribution = jnp.einsum("ri,cdit->cdrt", psi_rows, shifted_pmi_matrix, precision=highest)
        carry = carry + jnp.einsum("cdb,cdrt->rcdbt", chosen, partial_contribution, precision=highest)
        return carry, range_rows

    init = jnp.zeros((rank, N_COL, N_ROW, BPO, TILE), jnp.float32)
    corange, range_blocks = lax.scan(one_row, init, (tiles, live, select, row_sums, corange_test_blocks))
    range_sketch = range_blocks.transpose(1, 0, 2).reshape(rank, N_ROW * TILE)
    return (range_sketch, corange.reshape(rank, N_COL * N_ROW * BPO * TILE))
```

```python
import math

import jax
import jax.numpy as jnp
from jax import lax
from jax.experimental import pallas as pl
from jax.experimental.pallas import tpu as pltpu
from jax.sharding import PartitionSpec as P

shift_log = math.log(5.0)
LANES = 128
VMEM_LIMIT = 48 * 1024 * 1024
PARAMS = pltpu.CompilerParams(vmem_limit_bytes=VMEM_LIMIT)
SMEM = pl.BlockSpec(memory_space=pltpu.SMEM)
VMEM = pl.BlockSpec(memory_space=pltpu.VMEM)
ANY = pl.BlockSpec(memory_space=pl.ANY)

NN = (((1,), (0,)), ((), ()))
NT = (((1,), (1,)), ((), ()))


def f32(*shape):
    return jax.ShapeDtypeStruct(shape, jnp.float32)


def sums_kernel(pos_ref, counts_ref, packet_ref, row_ref):
    slots, tile, _ = counts_ref.shape
    ones = jnp.ones((8, tile), jnp.bfloat16)

    def eight(g, rows):
        columns = []
        for s in range(8):
            x = counts_ref[g * 8 + s]
            pos = pos_ref[g * 8 + s]
            live = pos >= 0
            column = lax.dot_general(ones, x, NN, preferred_element_type=jnp.float32)
            row = lax.dot_general(ones, x, NT, preferred_element_type=jnp.float32)
            at = jnp.full((1, LANES), pos.astype(jnp.float32))
            columns.append(jnp.concatenate([jnp.where(live, column[:1], 0.0), at], axis=1))
            rows = rows + jnp.where(live, row, 0.0)
        packet_ref[pl.ds(pl.multiple_of(g * 8, 8), 8), :] = jnp.concatenate(columns)
        return rows

    row_ref[...] = lax.fori_loop(0, slots // 8, eight, jnp.zeros((8, tile), jnp.float32))


def margin_kernel(blocks, me_ref, all_ref, row_ref, term_ref, swap_ref, incoming_ref):
    rows, slots, width = all_ref.shape
    tile = width - LANES

    def add(j, sums):
        value = all_ref[j, :, :tile]
        at = all_ref[j, :, tile:]
        at = jnp.concatenate([at] * (tile // LANES), axis=1)
        return tuple(sums[p] + jnp.where(at == p, value, 0.0) for p in range(blocks))

    zero = jnp.zeros((slots, tile), jnp.float32)
    sums = lax.fori_loop(0, rows, add, (zero,) * blocks, unroll=8)
    own = all_ref[0, :, tile:]
    own = jnp.concatenate([own] * (tile // LANES), axis=1)
    chosen = zero
    total = zero
    for p in range(blocks):
        power = jnp.exp(0.75 * jnp.log(jnp.maximum(sums[p], 1e-30)))
        total = total + jnp.where(sums[p] > 0.0, power, 0.0)
        chosen = chosen + jnp.where(own == p, sums[p], 0.0)
    term_ref[...] = jnp.where(own >= 0.0, -0.75 * jnp.log(jnp.maximum(chosen, 1e-30)), 0.0)
    total = sum(total[:, k * LANES : (k + 1) * LANES] for k in range(tile // LANES))
    total = sum(total[k * 8 : (k + 1) * 8] for k in range(slots // 8))
    swap_ref[:, :tile] = row_ref[...]
    swap_ref[:, tile:] = total
    mine = lax.broadcasted_iota(jnp.int32, (slots, LANES), 0) == me_ref[0]
    for j in range(rows):
        at = jnp.where(mine, all_ref[j, :, tile:], 0.0)
        incoming_ref[j : j + 1, :] = jnp.sum(at, axis=0, keepdims=True).astype(jnp.int32)


def matrix_kernel(me_ref, pos_ref, counts_ref, term_ref, mine_ref, other_ref, psi_ref, matrix_ref, *out_refs):
    slots, tile, _ = counts_ref.shape
    both = mine_ref[...] + other_ref[...]
    total = jnp.sum(both[:, tile:])
    shift = jnp.log(jnp.full((8, tile), total)) - jnp.log(both[:, :tile]) - shift_log
    shift = jnp.transpose(shift)[:, :1]

    def eight(g, carry):
        terms = term_ref[pl.ds(pl.multiple_of(g * 8, 8), 8), :]
        for k in range(8):
            s = g * 8 + k
            x = jnp.log(counts_ref[s].astype(jnp.float32))
            x = x + shift + terms[k : k + 1]
            x = jnp.where(pos_ref[s] >= 0, jnp.maximum(x, 0.0), 0.0)
            matrix_ref[s] = x.astype(jnp.bfloat16)
        return carry

    lax.fori_loop(0, slots // 8, eight, 0)
    psi = psi_ref[...]
    for k, out_ref in enumerate(out_refs):
        s = jnp.bitwise_xor(me_ref[0], k)
        out_ref[...] = lax.dot_general(psi, matrix_ref[s], NN, preferred_element_type=jnp.float32)


def range_kernel(blocks, pos_ref, matrix_ref, omega_ref, out_ref, chosen_ref, sems):
    slots, tile, _ = matrix_ref.shape

    def fetch(s):
        at = s * blocks + jnp.maximum(pos_ref[s], 0)
        columns = pl.ds(pl.multiple_of(at * tile, tile), tile)
        return pltpu.make_async_copy(omega_ref.at[:, columns], chosen_ref.at[s], sems.at[s])

    for s in range(slots):
        fetch(s).start()
    for s in range(slots):
        fetch(s).wait()
    out = jnp.zeros(out_ref.shape, jnp.float32)
    for s in range(slots):
        out = out + lax.dot_general(chosen_ref[s], matrix_ref[s], NT, preferred_element_type=jnp.float32)
    out_ref[...] = out


def place_kernel(at_ref, *refs):
    *in_refs, out_ref = refs
    tile = in_refs[0].shape[1]
    out_ref[...] = jnp.zeros_like(out_ref)
    for k, ref in enumerate(in_refs):
        p = at_ref[k, 0]

        @pl.when(p >= 0)
        def _():
            columns = pl.ds(pl.multiple_of(p * tile, tile), tile)
            out_ref[:, columns] += ref[...]


def on_device(counts, tile_pos, omega_t, psi):
    slots, tile, _ = counts.shape
    rank, width = omega_t.shape
    blocks = width // (slots * tile)
    rows = slots
    me = lax.axis_index("row").astype(jnp.int32).reshape(1)

    def row_xor(x, k):
        return lax.ppermute(x, "row", [(i, i ^ k) for i in range(rows)])

    def other_col(x):
        return lax.ppermute(x, "col", [(0, 1), (1, 0)])

    packet, row_part = pl.pallas_call(
        sums_kernel,
        out_shape=(f32(slots, tile + LANES), f32(8, tile)),
        in_specs=[SMEM, VMEM],
        out_specs=(VMEM, VMEM),
        compiler_params=PARAMS,
        name="sums",
    )(tile_pos, counts)

    gathered = packet[None]
    step = 1
    while step < rows:
        gathered = jnp.concatenate([gathered, row_xor(gathered, step)])
        step *= 2

    term, swap, incoming_at = pl.pallas_call(
        lambda *refs: margin_kernel(blocks, *refs),
        out_shape=(f32(slots, tile), f32(8, tile + LANES), jax.ShapeDtypeStruct((rows, LANES), jnp.int32)),
        in_specs=[SMEM, VMEM, VMEM],
        out_specs=(VMEM, VMEM, VMEM),
        compiler_params=PARAMS,
        name="margins",
    )(me, gathered, row_part)
    other = other_col(swap)

    matrix, *parts = pl.pallas_call(
        matrix_kernel,
        out_shape=(jax.ShapeDtypeStruct(counts.shape, jnp.bfloat16),) + (f32(rank, tile),) * rows,
        in_specs=[SMEM, SMEM] + [VMEM] * 5,
        out_specs=(VMEM,) * (rows + 1),
        compiler_params=PARAMS,
        name="matrix",
    )(me, tile_pos, counts, term, swap, other, psi)

    order = sorted(range(1, rows), key=lambda k: (-(k & -2), k))
    arrived = {0: parts[0]}
    for k in order:
        arrived[k] = row_xor(parts[k], k)

    partial_range = pl.pallas_call(
        lambda *refs: range_kernel(blocks, *refs),
        out_shape=f32(rank, tile),
        in_specs=[SMEM, VMEM, ANY],
        out_specs=VMEM,
        scratch_shapes=[pltpu.VMEM((slots, rank, tile), jnp.bfloat16), pltpu.SemaphoreType.DMA((slots,))],
        compiler_params=PARAMS,
        name="range",
    )(tile_pos, matrix, omega_t)
    range_sketch = partial_range + other_col(partial_range)

    corange = pl.pallas_call(
        place_kernel,
        out_shape=f32(rank, blocks * tile),
        in_specs=[SMEM] + [VMEM] * rows,
        out_specs=VMEM,
        compiler_params=PARAMS,
        name="place",
    )(incoming_at, *[arrived[k] for k in range(rows)])
    return (range_sketch, corange)


def solution(mesh):
    placed = (
        P(("grp", "row", "col"), None, None),
        P(("grp", "row", "col")),
        P(None, "col"),
        P(None, "row"),
    )
    return jax.shard_map(
        on_device,
        mesh=mesh,
        in_specs=placed,
        out_specs=(P(None, ("grp", "row")), P(None, ("grp", "col", "row"))),
        check_vma=False,
    )
```

```python
import math

import jax
import jax.numpy as jnp
from jax import lax
from jax.experimental import pallas as pl
from jax.experimental.pallas import tpu as pltpu
from jax.sharding import PartitionSpec as P

shift_log = math.log(5.0)
LANES = 128
EMPTY = -1e30
PARAMS = pltpu.CompilerParams(vmem_limit_bytes=40 * 1024 * 1024)
VMEM = pl.BlockSpec(memory_space=pltpu.VMEM)
HBM = pl.BlockSpec(memory_space=pltpu.HBM)

NN = (((1,), (0,)), ((), ()))
NT = (((1,), (1,)), ((), ()))


def f32(*shape):
    return jax.ShapeDtypeStruct(shape, jnp.float32)


def bf16(*shape):
    return jax.ShapeDtypeStruct(shape, jnp.bfloat16)


def sums_kernel(pos_hbm, counts_hbm, packet_ref, row_ref, counts_ref, pos_ref, pos_sem, sems):
    slots, tile, _ = counts_ref.shape
    fetch_pos = pltpu.make_async_copy(pos_hbm, pos_ref, pos_sem)
    fetch_pos.start()

    def fetch(s):
        return pltpu.make_async_copy(counts_hbm.at[s], counts_ref.at[s], sems.at[s])

    for s in range(slots):
        fetch(s).start()
    fetch_pos.wait()
    ones = jnp.ones((8, tile), jnp.bfloat16)

    def eight(g, rows):
        columns = []
        for k in range(8):
            s = g * 8 + k
            fetch(s).wait()
            x = counts_ref[s]
            pos = pos_ref[s]
            live = pos >= 0
            column = lax.dot_general(ones, x, NN, preferred_element_type=jnp.float32)
            row = lax.dot_general(ones, x, NT, preferred_element_type=jnp.float32)
            at = jnp.full((1, LANES), pos.astype(jnp.float32))
            columns.append(jnp.concatenate([jnp.where(live, column[:1], 0.0), at], axis=1))
            rows = rows + jnp.where(live, row, 0.0)
        packet_ref[pl.ds(pl.multiple_of(g * 8, 8), 8), :] = jnp.concatenate(columns)
        return rows

    rows = lax.fori_loop(0, slots // 8, eight, jnp.zeros((8, tile), jnp.float32))
    row_ref[...] = jnp.concatenate([rows, jnp.zeros((8, LANES), jnp.float32)], axis=1)


def prepare_kernel(blocks, pos_hbm, counts_ref, omega_hbm, psi_hbm, logs_ref, chosen_ref, psi_ref, pos_ref, sems):
    slots, tile, _ = counts_ref.shape
    fetch_pos = pltpu.make_async_copy(pos_hbm, pos_ref, sems.at[slots])
    fetch_psi = pltpu.make_async_copy(psi_hbm, psi_ref, sems.at[slots + 1])
    fetch_pos.start()
    fetch_psi.start()
    fetch_pos.wait()

    def fetch(s):
        at = s * blocks + jnp.maximum(pos_ref[s], 0)
        columns = pl.ds(pl.multiple_of(at * tile, tile), tile)
        return pltpu.make_async_copy(omega_hbm.at[:, columns], chosen_ref.at[s], sems.at[s])

    for s in range(slots):
        fetch(s).start()

    def one(s, carry):
        x = counts_ref[s].astype(jnp.float32)
        logs_ref[s] = jnp.log(jnp.where(pos_ref[s] >= 0, x, 1.0))
        return carry

    lax.fori_loop(0, slots, one, 0)
    for s in range(slots):
        fetch(s).wait()
    fetch_psi.wait()


def odd(r):
    return bin(r).count("1") % 2


def matrix_kernel(blocks, mine_ref, other_ref, logs_ref, psi_ref, matrix_ref, incoming_ref, *out_refs):
    slots, tile, _ = logs_ref.shape
    rows = slots
    wide = tile // LANES

    def column_sums(swapped):
        sums = [jnp.zeros((slots, tile), jnp.float32)] * blocks
        for r in range(rows):
            ref = other_ref if odd(r) != swapped else mine_ref
            value = ref[r * slots : (r + 1) * slots, :tile]
            at = ref[r * slots : (r + 1) * slots, tile:]
            at = jnp.concatenate([at] * wide, axis=1)
            sums = [s + jnp.where(at == p, value, 0.0) for p, s in enumerate(sums)]
        return sums

    def smooth_total(sums):
        total = jnp.zeros((slots, tile), jnp.float32)
        for s in sums:
            power = jnp.exp(0.75 * jnp.log(jnp.maximum(s, 1e-30)))
            total = total + jnp.where(s > 0.0, power, 0.0)
        return jnp.sum(total)

    sums = column_sums(False)
    first, second = smooth_total(sums), smooth_total(column_sums(True))
    total = first + second
    own = mine_ref[:slots, tile:]
    own = jnp.concatenate([own] * wide, axis=1)
    chosen = jnp.zeros((slots, tile), jnp.float32)
    for p in range(blocks):
        chosen = chosen + jnp.where(own == p, sums[p], 0.0)
    terms = jnp.where(own >= 0.0, -0.75 * jnp.log(jnp.maximum(chosen, 1e-30)), EMPTY)

    me = lax.axis_index("row")
    mine = lax.broadcasted_iota(jnp.int32, (slots, LANES), 0) == me
    for r in range(rows):
        ref = other_ref if odd(r) else mine_ref
        at = jnp.where(mine, ref[r * slots : (r + 1) * slots, tile:], 0.0)
        incoming_ref[r : r + 1, :] = jnp.sum(at, axis=0, keepdims=True).astype(jnp.int32)

    both = mine_ref[rows * slots :, :tile] + other_ref[rows * slots :, :tile]
    shift = jnp.log(jnp.full((8, tile), total)) - jnp.log(both) - shift_log
    shift = jnp.transpose(shift)[:, :1]

    for s in range(slots):
        x = logs_ref[s] + shift + terms[s : s + 1]
        matrix_ref[s] = jnp.maximum(x, 0.0).astype(jnp.bfloat16)
    psi = psi_ref[...]
    for k, out_ref in enumerate(out_refs):
        s = jnp.bitwise_xor(me, k)
        out_ref[...] = lax.dot_general(psi, matrix_ref[s], NN, preferred_element_type=jnp.float32)


def place(at_ref, refs, first, out_ref):
    tile = refs[0].shape[1]
    for k, ref in zip(first, refs, strict=True):
        p = at_ref[k, 0]

        @pl.when(p >= 0)
        def _():
            columns = pl.ds(pl.multiple_of(p * tile, tile), tile)
            out_ref[:, columns] += ref[...]


def early_kernel(order, at_ref, matrix_ref, chosen_ref, *refs):
    *in_refs, range_ref, out_ref = refs
    out = jnp.zeros(range_ref.shape, jnp.float32)
    for s in range(matrix_ref.shape[0]):
        out = out + lax.dot_general(chosen_ref[s], matrix_ref[s], NT, preferred_element_type=jnp.float32)
    range_ref[...] = out
    out_ref[...] = jnp.zeros_like(out_ref)
    place(at_ref, in_refs, order, out_ref)


def late_kernel(order, at_ref, early_ref, mine_ref, other_ref, *refs):
    *in_refs, range_hbm, out_hbm, range_ref, out_ref, sems = refs
    out_ref[...] = early_ref[...]
    place(at_ref, in_refs, order, out_ref)
    range_ref[...] = mine_ref[...] + other_ref[...]
    rank = out_ref.shape[0]
    copies = [pltpu.make_async_copy(range_ref, range_hbm, sems.at[rank // 8])]
    for k in range(rank // 8):
        some = pl.ds(k * 8, 8)
        copies.append(pltpu.make_async_copy(out_ref.at[some], out_hbm.at[some], sems.at[k]))
    for copy in copies:
        copy.start()
    for copy in copies:
        copy.wait()


def on_device(counts, tile_pos, omega_t, psi):
    slots, tile, _ = counts.shape
    rank, width = omega_t.shape
    blocks = width // (slots * tile)
    rows = slots
    DMA = pltpu.SemaphoreType.DMA

    def call(kernel, name, outs, ins, out_specs=None, scratch=(), cost=None):
        return pl.pallas_call(
            kernel,
            out_shape=outs,
            in_specs=ins,
            out_specs=out_specs or (VMEM,) * len(outs),
            scratch_shapes=scratch,
            compiler_params=PARAMS,
            cost_estimate=cost,
            name=name,
        )

    def row_xor(x, k):
        return lax.ppermute(x, "row", [(i, i ^ k) for i in range(rows)])

    def across(x, k):
        pairs = [(2 * i + c, 2 * (i ^ k) + 1 - c) for i in range(rows) for c in range(2)]
        return lax.ppermute(x, ("row", "col"), pairs)

    def other_col(x):
        return lax.ppermute(x, "col", [(0, 1), (1, 0)])

    counts, tile_pos, omega_t, psi = (
        pltpu.with_memory_space_constraint(x, pltpu.HBM) for x in (counts, tile_pos, omega_t, psi)
    )
    packet, row_part, held = call(
        sums_kernel,
        "sums",
        (f32(slots, tile + LANES), f32(8, tile + LANES), bf16(slots, tile, tile)),
        [HBM, HBM],
        scratch=[pltpu.SMEM((slots,), jnp.int32), DMA(()), DMA((slots,))],
    )(tile_pos, counts)

    logs, chosen, held_psi = call(
        lambda *refs: prepare_kernel(blocks, *refs),
        "prepare",
        (f32(slots, tile, tile), bf16(slots, rank, tile), bf16(*psi.shape)),
        [HBM, VMEM, HBM, HBM],
        scratch=[pltpu.SMEM((slots,), jnp.int32), DMA((slots + 2,))],
        cost=pl.CostEstimate(flops=40 * counts.size, bytes_accessed=6 * counts.size, transcendentals=counts.size),
    )(tile_pos, held, omega_t, psi)

    gathered = packet
    step = 1
    while step < rows:
        gathered = jnp.concatenate([gathered, across(gathered, step)])
        step *= 2
    gathered = jnp.concatenate([gathered, row_part])
    gathered, logs, chosen, held_psi = lax.optimization_barrier((gathered, logs, chosen, held_psi))
    other = other_col(gathered)

    matrix, incoming_at, *parts = call(
        lambda *refs: matrix_kernel(blocks, *refs),
        "matrix",
        (bf16(*counts.shape), jax.ShapeDtypeStruct((rows, LANES), jnp.int32)) + (f32(rank, tile),) * rows,
        [VMEM] * 4,
    )(gathered, other, logs, held_psi)

    order = sorted(range(1, rows), key=lambda k: (-(k & -2), k))
    arrived = [row_xor(parts[k], k) for k in order]
    half = (rows - 1) // 2
    at = pl.BlockSpec(memory_space=pltpu.SMEM)

    partial_range, early = call(
        lambda *refs: early_kernel([0] + order[:half], *refs),
        "early",
        (f32(rank, tile), f32(rank, blocks * tile)),
        [at] + [VMEM] * (3 + half),
    )(incoming_at, matrix, chosen, parts[0], *arrived[:half])
    other_range = other_col(partial_range)
    return call(
        lambda *refs: late_kernel(order[half:], *refs),
        "late",
        (f32(rank, tile), f32(rank, blocks * tile)),
        [at] + [VMEM] * (3 + rows - 1 - half),
        out_specs=(HBM, HBM),
        scratch=[pltpu.VMEM((rank, tile), jnp.float32), pltpu.VMEM((rank, blocks * tile), jnp.float32), DMA((rank // 8 + 1,))],
    )(incoming_at, early, partial_range, other_range, *arrived[half:])


def solution(mesh):
    placed = (
        P(("grp", "row", "col"), None, None),
        P(("grp", "row", "col")),
        P(None, "col"),
        P(None, "row"),
    )
    return jax.shard_map(
        on_device,
        mesh=mesh,
        in_specs=placed,
        out_specs=(P(None, ("grp", "row")), P(None, ("grp", "col", "row"))),
        check_vma=False,
    )
```

```python
import math

import jax
import jax.numpy as jnp
from jax import lax
from jax.experimental import pallas as pl
from jax.experimental.pallas import tpu as pltpu
from jax.sharding import PartitionSpec as P

shift_log = math.log(5.0)
LANES = 128
EMPTY = -1e30
PARAMS = pltpu.CompilerParams(vmem_limit_bytes=40 * 1024 * 1024)
VMEM = pl.BlockSpec(memory_space=pltpu.VMEM)
HBM = pl.BlockSpec(memory_space=pltpu.HBM)

NN = (((1,), (0,)), ((), ()))
NT = (((1,), (1,)), ((), ()))


def f32(*shape):
    return jax.ShapeDtypeStruct(shape, jnp.float32)


def bf16(*shape):
    return jax.ShapeDtypeStruct(shape, jnp.bfloat16)


def sums_kernel(pos_hbm, counts_hbm, packet_ref, row_ref, counts_ref, pos_ref, pos_sem, sems):
    slots, tile, _ = counts_ref.shape
    fetch_pos = pltpu.make_async_copy(pos_hbm, pos_ref, pos_sem)
    fetch_pos.start()
    fetches = [pltpu.make_async_copy(counts_hbm.at[s], counts_ref.at[s], sems.at[s]) for s in range(slots)]
    for fetch in fetches:
        fetch.start()
    fetch_pos.wait()

    values = jnp.zeros((tile, tile), jnp.float32)
    for g in range(0, slots, 8):
        columns = []
        for s in range(g, g + 8):
            fetches[s].wait()
            x = jnp.where(pos_ref[s] >= 0, counts_ref[s].astype(jnp.float32), 0.0)
            at = jnp.full((1, LANES), pos_ref[s].astype(jnp.float32))
            columns.append(jnp.concatenate([jnp.sum(x, axis=0, keepdims=True), at], axis=1))
            values = values + x
        packet_ref[g : g + 8, :] = jnp.concatenate(columns)
    narrow = sum(values[:, k : k + LANES] for k in range(0, tile, LANES))
    rows = jnp.sum(jnp.transpose(narrow), axis=0, keepdims=True)
    row_ref[:, :tile] = jnp.broadcast_to(rows, (8, tile))
    row_ref[:, tile:] = jnp.zeros((8, LANES), jnp.float32)


def prepare_kernel(blocks, pos_hbm, counts_ref, omega_hbm, psi_hbm, logs_ref, chosen_ref, psi_ref, pos_ref, sems):
    slots, tile, _ = counts_ref.shape
    fetch_pos = pltpu.make_async_copy(pos_hbm, pos_ref, sems.at[slots])
    fetch_psi = pltpu.make_async_copy(psi_hbm, psi_ref, sems.at[slots + 1])
    fetch_pos.start()
    fetch_psi.start()
    fetch_pos.wait()

    def fetch(s):
        at = s * blocks + jnp.maximum(pos_ref[s], 0)
        columns = pl.ds(pl.multiple_of(at * tile, tile), tile)
        return pltpu.make_async_copy(omega_hbm.at[:, columns], chosen_ref.at[s], sems.at[s])

    for s in range(slots):
        fetch(s).start()

    def one(s, carry):
        x = counts_ref[s].astype(jnp.float32)
        logs_ref[s] = jnp.log(jnp.where(pos_ref[s] >= 0, x, 1.0))
        return carry

    lax.fori_loop(0, slots, one, 0)
    for s in range(slots):
        fetch(s).wait()
    fetch_psi.wait()


def stages(rows):
    bits = [1 << k for k in range(2, rows.bit_length() - 1)]
    return [[(1, 1), (2, 1), (3, 0)]] + [[(bit, 1)] for bit in bits]


def matrix_kernel(blocks, offsets, mine_ref, other_ref, logs_ref, psi_ref, matrix_ref, incoming_ref, *out_refs):
    slots, tile, _ = logs_ref.shape
    rows = slots
    wide = tile // LANES

    def column_sums(swapped):
        sums = [jnp.zeros((slots, tile), jnp.float32)] * blocks
        for k, (_, c) in enumerate(offsets):
            ref = other_ref if c != swapped else mine_ref
            value = ref[k * slots : (k + 1) * slots, :tile]
            at = ref[k * slots : (k + 1) * slots, tile:]
            at = jnp.concatenate([at] * wide, axis=1)
            sums = [s + jnp.where(at == p, value, 0.0) for p, s in enumerate(sums)]
        return sums

    def smooth_total(sums):
        total = jnp.zeros((slots, tile), jnp.float32)
        for s in sums:
            power = jnp.exp(0.75 * jnp.log(jnp.maximum(s, 1e-30)))
            total = total + jnp.where(s > 0.0, power, 0.0)
        return jnp.sum(total)

    sums = column_sums(0)
    first, second = smooth_total(sums), smooth_total(column_sums(1))
    total = first + second
    own = mine_ref[:slots, tile:]
    own = jnp.concatenate([own] * wide, axis=1)
    chosen = jnp.zeros((slots, tile), jnp.float32)
    for p in range(blocks):
        chosen = chosen + jnp.where(own == p, sums[p], 0.0)
    terms = jnp.where(own >= 0.0, -0.75 * jnp.log(jnp.maximum(chosen, 1e-30)), EMPTY)

    me = lax.axis_index("row")
    mine = lax.broadcasted_iota(jnp.int32, (slots, LANES), 0) == me
    for k, (r, c) in enumerate(offsets):
        ref = other_ref if c else mine_ref
        at = jnp.where(mine, ref[k * slots : (k + 1) * slots, tile:], 0.0)
        incoming_ref[r : r + 1, :] = jnp.sum(at, axis=0, keepdims=True).astype(jnp.int32)

    both = mine_ref[rows * slots :, :tile] + other_ref[rows * slots :, :tile]
    shift = jnp.log(jnp.full((8, tile), total)) - jnp.log(both) - shift_log
    shift = jnp.transpose(shift)[:, :1]

    for s in range(slots):
        x = logs_ref[s] + shift + terms[s : s + 1]
        matrix_ref[s] = jnp.maximum(x, 0.0).astype(jnp.bfloat16)
    psi = psi_ref[...]
    for k, out_ref in enumerate(out_refs):
        s = jnp.bitwise_xor(me, k)
        out_ref[...] = lax.dot_general(psi, matrix_ref[s], NN, preferred_element_type=jnp.float32)


def place(at_ref, refs, first, out_ref):
    tile = refs[0].shape[1]
    at = [jnp.max(at_ref[k : k + 1, :]) for k in first]
    for p, ref in zip(at, refs, strict=True):
        columns = pl.ds(pl.multiple_of(jnp.maximum(p, 0) * tile, tile), tile)
        out_ref[:, columns] += jnp.where(p >= 0, ref[...], 0.0)


def early_kernel(order, at_ref, matrix_ref, chosen_ref, *refs):
    *in_refs, range_ref, out_ref = refs
    out = jnp.zeros(range_ref.shape, jnp.float32)
    for s in range(matrix_ref.shape[0]):
        out = out + lax.dot_general(chosen_ref[s], matrix_ref[s], NT, preferred_element_type=jnp.float32)
    range_ref[...] = out
    out_ref[...] = jnp.zeros_like(out_ref)
    place(at_ref, in_refs, order, out_ref)


def late_kernel(order, at_ref, early_ref, mine_ref, other_ref, *refs):
    *in_refs, range_hbm, out_hbm, range_ref, out_ref, sems = refs
    out_ref[...] = early_ref[...]
    place(at_ref, in_refs, order, out_ref)
    range_ref[...] = mine_ref[...] + other_ref[...]
    rank = out_ref.shape[0]
    copies = [pltpu.make_async_copy(range_ref, range_hbm, sems.at[rank // 8])]
    for k in range(rank // 8):
        some = pl.ds(k * 8, 8)
        copies.append(pltpu.make_async_copy(out_ref.at[some], out_hbm.at[some], sems.at[k]))
    for copy in copies:
        copy.start()
    for copy in copies:
        copy.wait()


def on_device(counts, tile_pos, omega_t, psi):
    slots, tile, _ = counts.shape
    rank, width = omega_t.shape
    blocks = width // (slots * tile)
    rows = slots
    DMA = pltpu.SemaphoreType.DMA

    def call(kernel, name, outs, ins, out_specs=None, scratch=(), cost=None):
        return pl.pallas_call(
            kernel,
            out_shape=outs,
            in_specs=ins,
            out_specs=out_specs or (VMEM,) * len(outs),
            scratch_shapes=scratch,
            compiler_params=PARAMS,
            cost_estimate=cost,
            name=name,
        )

    def row_xor(x, k):
        return lax.ppermute(x, "row", [(i, i ^ k) for i in range(rows)])

    def across(x, k, odd):
        pairs = [(2 * i + c, 2 * (i ^ k) + (c ^ odd)) for i in range(rows) for c in range(2)]
        return lax.ppermute(x, ("row", "col"), pairs)

    def other_col(x):
        return lax.ppermute(x, "col", [(0, 1), (1, 0)])

    counts, tile_pos, omega_t, psi = (
        pltpu.with_memory_space_constraint(x, pltpu.HBM) for x in (counts, tile_pos, omega_t, psi)
    )
    packet, row_part, held = call(
        sums_kernel,
        "sums",
        (f32(slots, tile + LANES), f32(8, tile + LANES), bf16(slots, tile, tile)),
        [HBM, HBM],
        scratch=[pltpu.SMEM((slots,), jnp.int32), DMA(()), DMA((slots,))],
    )(tile_pos, counts)

    logs, chosen, held_psi = call(
        lambda *refs: prepare_kernel(blocks, *refs),
        "prepare",
        (f32(slots, tile, tile), bf16(slots, rank, tile), bf16(*psi.shape)),
        [HBM, VMEM, HBM, HBM],
        scratch=[pltpu.SMEM((slots,), jnp.int32), DMA((slots + 2,))],
        cost=pl.CostEstimate(flops=40 * counts.size, bytes_accessed=6 * counts.size, transcendentals=counts.size),
    )(tile_pos, held, omega_t, psi)

    gathered = packet
    offsets = [(0, 0)]
    for stage in stages(rows):
        sent = [across(gathered, k, odd) for k, odd in stage]
        gathered = jnp.concatenate([gathered] + sent)
        offsets += [(r ^ k, c ^ odd) for k, odd in stage for r, c in offsets]
    gathered = jnp.concatenate([gathered, row_part])
    gathered, logs, chosen, held_psi = lax.optimization_barrier((gathered, logs, chosen, held_psi))
    other = other_col(gathered)

    matrix, incoming_at, *parts = call(
        lambda *refs: matrix_kernel(blocks, offsets, *refs),
        "matrix",
        (bf16(*counts.shape), jax.ShapeDtypeStruct((rows, LANES), jnp.int32)) + (f32(rank, tile),) * rows,
        [VMEM] * 4,
    )(gathered, other, logs, held_psi)

    order = list(range(rows - 1, 0, -1))
    arrived = [row_xor(parts[k], k) for k in order]
    half = 2

    partial_range, early = call(
        lambda *refs: early_kernel([0] + order[:half], *refs),
        "early",
        (f32(rank, tile), f32(rank, blocks * tile)),
        [VMEM] * (4 + half),
    )(incoming_at, matrix, chosen, parts[0], *arrived[:half])
    other_range = other_col(partial_range)
    return call(
        lambda *refs: late_kernel(order[half:], *refs),
        "late",
        (f32(rank, tile), f32(rank, blocks * tile)),
        [VMEM] * (4 + rows - 1 - half),
        out_specs=(HBM, HBM),
        scratch=[pltpu.VMEM((rank, tile), jnp.float32), pltpu.VMEM((rank, blocks * tile), jnp.float32), DMA((rank // 8 + 1,))],
    )(incoming_at, early, partial_range, other_range, *arrived[half:])


def solution(mesh):
    placed = (
        P(("grp", "row", "col"), None, None),
        P(("grp", "row", "col")),
        P(None, "col"),
        P(None, "row"),
    )
    return jax.shard_map(
        on_device,
        mesh=mesh,
        in_specs=placed,
        out_specs=(P(None, ("grp", "row")), P(None, ("grp", "col", "row"))),
        check_vma=False,
    )
```

```python
import math

import jax
import jax.numpy as jnp
from jax import lax
from jax.experimental import pallas as pl
from jax.experimental.pallas import tpu as pltpu
from jax.sharding import PartitionSpec as P

shift_log = math.log(5.0)
LANES = 128
EMPTY = -1e30
PARAMS = pltpu.CompilerParams(vmem_limit_bytes=40 * 1024 * 1024)
VMEM = pl.BlockSpec(memory_space=pltpu.VMEM)
HBM = pl.BlockSpec(memory_space=pltpu.HBM)

NN = (((1,), (0,)), ((), ()))
NT = (((1,), (1,)), ((), ()))


def f32(*shape):
    return jax.ShapeDtypeStruct(shape, jnp.float32)


def bf16(*shape):
    return jax.ShapeDtypeStruct(shape, jnp.bfloat16)


def sums_kernel(pos_hbm, counts_hbm, packet_ref, row_ref, counts_ref, pos_ref, pos_sem, sems):
    slots, tile, _ = counts_ref.shape
    fetch_pos = pltpu.make_async_copy(pos_hbm, pos_ref, pos_sem)
    fetch_pos.start()
    fetches = [pltpu.make_async_copy(counts_hbm.at[s], counts_ref.at[s], sems.at[s]) for s in range(slots)]
    for fetch in fetches:
        fetch.start()
    fetch_pos.wait()

    values = jnp.zeros((tile, tile), jnp.float32)
    for g in range(0, slots, 8):
        columns = []
        for s in range(g, g + 8):
            fetches[s].wait()
            x = jnp.where(pos_ref[s] >= 0, counts_ref[s].astype(jnp.float32), 0.0)
            at = jnp.full((1, LANES), pos_ref[s].astype(jnp.float32))
            columns.append(jnp.concatenate([jnp.sum(x, axis=0, keepdims=True), at], axis=1))
            values = values + x
        packet_ref[g : g + 8, :] = jnp.concatenate(columns)
    narrow = sum(values[:, k : k + LANES] for k in range(0, tile, LANES))
    rows = jnp.sum(jnp.transpose(narrow), axis=0, keepdims=True)
    row_ref[:, :tile] = jnp.broadcast_to(rows, (8, tile))
    row_ref[:, tile:] = jnp.zeros((8, LANES), jnp.float32)


def prepare_kernel(blocks, pos_hbm, counts_ref, omega_hbm, psi_hbm, logs_ref, chosen_ref, psi_ref, pos_ref, sems):
    slots, tile, _ = counts_ref.shape
    fetch_pos = pltpu.make_async_copy(pos_hbm, pos_ref, sems.at[slots])
    fetch_psi = pltpu.make_async_copy(psi_hbm, psi_ref, sems.at[slots + 1])
    fetch_pos.start()
    fetch_psi.start()
    fetch_pos.wait()

    def fetch(s):
        at = s * blocks + jnp.maximum(pos_ref[s], 0)
        columns = pl.ds(pl.multiple_of(at * tile, tile), tile)
        return pltpu.make_async_copy(omega_hbm.at[:, columns], chosen_ref.at[s], sems.at[s])

    for s in range(slots):
        fetch(s).start()

    def one(s, carry):
        x = counts_ref[s].astype(jnp.float32)
        logs_ref[s] = jnp.log(jnp.where(pos_ref[s] >= 0, x, 1.0))
        return carry

    lax.fori_loop(0, slots, one, 0)
    for s in range(slots):
        fetch(s).wait()
    fetch_psi.wait()


def stages(rows):
    bits = [1 << k for k in range(2, rows.bit_length() - 1)]
    return [[(1, 1), (2, 1), (3, 0)]] + [[(bit, 1)] for bit in bits]


def send_order(rows):
    half = rows // 2
    far, near = list(range(rows - 1, half - 1, -1)), list(range(half - 1, 0, -1))
    late = [k for pair in zip(near, far[2:]) for k in pair]
    return far[:2] + late + near[len(far) - 2 :]


def matrix_kernel(blocks, offsets, mine_ref, other_ref, logs_ref, psi_ref, matrix_ref, incoming_ref, *out_refs):
    slots, tile, _ = logs_ref.shape
    rows = slots
    wide = tile // LANES

    def column_sums(swapped):
        sums = [jnp.zeros((slots, tile), jnp.float32)] * blocks
        for k, (_, c) in enumerate(offsets):
            ref = other_ref if c != swapped else mine_ref
            value = ref[k * slots : (k + 1) * slots, :tile]
            at = ref[k * slots : (k + 1) * slots, tile:]
            at = jnp.concatenate([at] * wide, axis=1)
            sums = [s + jnp.where(at == p, value, 0.0) for p, s in enumerate(sums)]
        return sums

    def smooth_total(sums):
        total = jnp.zeros((slots, tile), jnp.float32)
        for s in sums:
            power = jnp.exp(0.75 * jnp.log(jnp.maximum(s, 1e-30)))
            total = total + jnp.where(s > 0.0, power, 0.0)
        return jnp.sum(total)

    sums = column_sums(0)
    first, second = smooth_total(sums), smooth_total(column_sums(1))
    total = first + second
    own = mine_ref[:slots, tile:]
    own = jnp.concatenate([own] * wide, axis=1)
    chosen = jnp.zeros((slots, tile), jnp.float32)
    for p in range(blocks):
        chosen = chosen + jnp.where(own == p, sums[p], 0.0)
    terms = jnp.where(own >= 0.0, -0.75 * jnp.log(jnp.maximum(chosen, 1e-30)), EMPTY)

    me = lax.axis_index("row")
    mine = lax.broadcasted_iota(jnp.int32, (slots, LANES), 0) == me
    for k, (r, c) in enumerate(offsets):
        ref = other_ref if c else mine_ref
        at = jnp.where(mine, ref[k * slots : (k + 1) * slots, tile:], 0.0)
        incoming_ref[r : r + 1, :] = jnp.sum(at, axis=0, keepdims=True).astype(jnp.int32)

    both = mine_ref[rows * slots :, :tile] + other_ref[rows * slots :, :tile]
    shift = jnp.log(jnp.full((8, tile), total)) - jnp.log(both) - shift_log
    shift = jnp.transpose(shift)[:, :1]

    for s in range(slots):
        x = logs_ref[s] + shift + terms[s : s + 1]
        matrix_ref[s] = jnp.maximum(x, 0.0).astype(jnp.bfloat16)
    psi = psi_ref[...]
    for k, out_ref in enumerate(out_refs):
        s = jnp.bitwise_xor(me, k)
        out_ref[...] = lax.dot_general(psi, matrix_ref[s], NN, preferred_element_type=jnp.float32)


def place(at_ref, refs, first, out_ref):
    tile = refs[0].shape[1]
    at = [jnp.max(at_ref[k : k + 1, :]) for k in first]
    for p, ref in zip(at, refs, strict=True):
        columns = pl.ds(pl.multiple_of(jnp.maximum(p, 0) * tile, tile), tile)
        out_ref[:, columns] += jnp.where(p >= 0, ref[...], 0.0)


def early_kernel(order, at_ref, matrix_ref, chosen_ref, *refs):
    *in_refs, range_ref, out_ref = refs
    out = jnp.zeros(range_ref.shape, jnp.float32)
    for s in range(matrix_ref.shape[0]):
        out = out + lax.dot_general(chosen_ref[s], matrix_ref[s], NT, preferred_element_type=jnp.float32)
    range_ref[...] = out
    out_ref[...] = jnp.zeros_like(out_ref)
    place(at_ref, in_refs, order, out_ref)


def late_kernel(order, at_ref, early_ref, mine_ref, other_ref, *refs):
    *in_refs, range_hbm, out_hbm, range_ref, out_ref, sems = refs
    out_ref[...] = early_ref[...]
    place(at_ref, in_refs, order, out_ref)
    range_ref[...] = mine_ref[...] + other_ref[...]
    rank = out_ref.shape[0]
    copies = [pltpu.make_async_copy(range_ref, range_hbm, sems.at[rank // 8])]
    for k in range(rank // 8):
        some = pl.ds(k * 8, 8)
        copies.append(pltpu.make_async_copy(out_ref.at[some], out_hbm.at[some], sems.at[k]))
    for copy in copies:
        copy.start()
    for copy in copies:
        copy.wait()


def on_device(counts, tile_pos, omega_t, psi):
    slots, tile, _ = counts.shape
    rank, width = omega_t.shape
    blocks = width // (slots * tile)
    rows = slots
    DMA = pltpu.SemaphoreType.DMA

    def call(kernel, name, outs, ins, out_specs=None, scratch=(), cost=None):
        return pl.pallas_call(
            kernel,
            out_shape=outs,
            in_specs=ins,
            out_specs=out_specs or (VMEM,) * len(outs),
            scratch_shapes=scratch,
            compiler_params=PARAMS,
            cost_estimate=cost,
            name=name,
        )

    def row_xor(x, k):
        return lax.ppermute(x, "row", [(i, i ^ k) for i in range(rows)])

    def across(x, k, odd):
        pairs = [(2 * i + c, 2 * (i ^ k) + (c ^ odd)) for i in range(rows) for c in range(2)]
        return lax.ppermute(x, ("row", "col"), pairs)

    def other_col(x):
        return lax.ppermute(x, "col", [(0, 1), (1, 0)])

    counts, tile_pos, omega_t, psi = (
        pltpu.with_memory_space_constraint(x, pltpu.HBM) for x in (counts, tile_pos, omega_t, psi)
    )
    packet, row_part, held = call(
        sums_kernel,
        "sums",
        (f32(slots, tile + LANES), f32(8, tile + LANES), bf16(slots, tile, tile)),
        [HBM, HBM],
        scratch=[pltpu.SMEM((slots,), jnp.int32), DMA(()), DMA((slots,))],
    )(tile_pos, counts)

    gathered = packet
    offsets = [(0, 0)]
    for stage in stages(rows):
        gathered, held = lax.optimization_barrier((gathered, held))
        sent = [across(gathered, k, odd) for k, odd in stage]
        gathered = jnp.concatenate([gathered] + sent)
        offsets += [(r ^ k, c ^ odd) for k, odd in stage for r, c in offsets]
    logs, chosen, held_psi = call(
        lambda *refs: prepare_kernel(blocks, *refs),
        "prepare",
        (f32(slots, tile, tile), bf16(slots, rank, tile), bf16(*psi.shape)),
        [HBM, VMEM, HBM, HBM],
        scratch=[pltpu.SMEM((slots,), jnp.int32), DMA((slots + 2,))],
        cost=pl.CostEstimate(flops=40 * counts.size, bytes_accessed=6 * counts.size, transcendentals=counts.size),
    )(tile_pos, held, omega_t, psi)

    gathered = jnp.concatenate([gathered, row_part])
    gathered, logs, chosen, held_psi = lax.optimization_barrier((gathered, logs, chosen, held_psi))
    other = other_col(gathered)

    matrix, incoming_at, *parts = call(
        lambda *refs: matrix_kernel(blocks, offsets, *refs),
        "matrix",
        (bf16(*counts.shape), jax.ShapeDtypeStruct((rows, LANES), jnp.int32)) + (f32(rank, tile),) * rows,
        [VMEM] * 4,
    )(gathered, other, logs, held_psi)

    order = send_order(rows)
    arrived = [row_xor(parts[k], k) for k in order]
    half = 2

    partial_range, early = call(
        lambda *refs: early_kernel([0] + order[:half], *refs),
        "early",
        (f32(rank, tile), f32(rank, blocks * tile)),
        [VMEM] * (4 + half),
    )(incoming_at, matrix, chosen, parts[0], *arrived[:half])
    other_range = other_col(partial_range)
    return call(
        lambda *refs: late_kernel(order[half:], *refs),
        "late",
        (f32(rank, tile), f32(rank, blocks * tile)),
        [VMEM] * (4 + rows - 1 - half),
        out_specs=(HBM, HBM),
        scratch=[pltpu.VMEM((rank, tile), jnp.float32), pltpu.VMEM((rank, blocks * tile), jnp.float32), DMA((rank // 8 + 1,))],
    )(incoming_at, early, partial_range, other_range, *arrived[half:])


def solution(mesh):
    placed = (
        P(("grp", "row", "col"), None, None),
        P(("grp", "row", "col")),
        P(None, "col"),
        P(None, "row"),
    )
    return jax.shard_map(
        on_device,
        mesh=mesh,
        in_specs=placed,
        out_specs=(P(None, ("grp", "row")), P(None, ("grp", "col", "row"))),
        check_vma=False,
    )
```

```python
import math

import jax
import jax.numpy as jnp
from jax import lax
from jax.experimental import pallas as pl
from jax.experimental.pallas import tpu as pltpu
from jax.sharding import PartitionSpec as P

shift_log = math.log(5.0)
LANES = 128
EMPTY = -1e30
PARAMS = pltpu.CompilerParams(vmem_limit_bytes=40 * 1024 * 1024)
VMEM = pl.BlockSpec(memory_space=pltpu.VMEM)
HBM = pl.BlockSpec(memory_space=pltpu.HBM)

NN = (((1,), (0,)), ((), ()))
NT = (((1,), (1,)), ((), ()))


def f32(*shape):
    return jax.ShapeDtypeStruct(shape, jnp.float32)


def bf16(*shape):
    return jax.ShapeDtypeStruct(shape, jnp.bfloat16)


def sums_kernel(pos_hbm, counts_hbm, packet_ref, row_ref, counts_ref, pos_ref, pos_sem, sems):
    slots, tile, _ = counts_ref.shape
    fetch_pos = pltpu.make_async_copy(pos_hbm, pos_ref, pos_sem)
    fetch_pos.start()
    fetches = [pltpu.make_async_copy(counts_hbm.at[s], counts_ref.at[s], sems.at[s]) for s in range(slots)]
    for fetch in fetches:
        fetch.start()
    fetch_pos.wait()

    values = jnp.zeros((tile, tile), jnp.float32)
    for g in range(0, slots, 8):
        columns = []
        for s in range(g, g + 8):
            fetches[s].wait()
            x = jnp.where(pos_ref[s] >= 0, counts_ref[s].astype(jnp.float32), 0.0)
            at = jnp.full((1, LANES), pos_ref[s].astype(jnp.float32))
            columns.append(jnp.concatenate([jnp.sum(x, axis=0, keepdims=True), at], axis=1))
            values = values + x
        packet_ref[g : g + 8, :] = jnp.concatenate(columns)
    narrow = sum(values[:, k : k + LANES] for k in range(0, tile, LANES))
    rows = jnp.sum(jnp.transpose(narrow), axis=0, keepdims=True)
    row_ref[...] = jnp.broadcast_to(rows, (8, tile))


def prepare_kernel(blocks, pos_hbm, counts_ref, omega_hbm, psi_hbm, logs_ref, chosen_ref, psi_ref, pos_ref, sems):
    slots, tile, _ = counts_ref.shape
    fetch_pos = pltpu.make_async_copy(pos_hbm, pos_ref, sems.at[slots])
    fetch_psi = pltpu.make_async_copy(psi_hbm, psi_ref, sems.at[slots + 1])
    fetch_pos.start()
    fetch_psi.start()
    fetch_pos.wait()

    def fetch(s):
        at = s * blocks + jnp.maximum(pos_ref[s], 0)
        columns = pl.ds(pl.multiple_of(at * tile, tile), tile)
        return pltpu.make_async_copy(omega_hbm.at[:, columns], chosen_ref.at[s], sems.at[s])

    for s in range(slots):
        fetch(s).start()

    def one(s, carry):
        x = counts_ref[s].astype(jnp.float32)
        logs_ref[s] = jnp.log(jnp.where(pos_ref[s] >= 0, x, 1.0))
        return carry

    lax.fori_loop(0, slots, one, 0)
    for s in range(slots):
        fetch(s).wait()
    fetch_psi.wait()


def stages(rows):
    bits = [1 << k for k in range(2, rows.bit_length() - 1)]
    return [[(1, 1), (2, 1), (3, 0)]] + [[(bit, 1)] for bit in bits]


def outer(row):
    return ((row >> 2) ^ (row >> 1)) & 1 == 0


def rounds(rows):
    if rows == 8:
        return [(4, 4), (6, 1), (7, 7), (3, 3), (5, 5), (2, 2), (1, 6)]
    return [(k, k) for k in range(rows - 1, 0, -1)]


def matrix_kernel(blocks, near, far, order, mine_ref, other_ref, logs_ref, psi_ref, matrix_ref, incoming_ref, *out_refs):
    slots, tile, _ = logs_ref.shape
    rows = slots
    group = LANES // len(near)
    packets = {}
    for g, (r, c) in enumerate(far):
        some = slice(g * slots, (g + 1) * slots)
        for j, (r2, c2) in enumerate(near):
            for core, ref in enumerate((mine_ref, other_ref)):
                at = ref[some, len(near) * tile + j * group :][:, :1]
                value = ref[some, j * tile : (j + 1) * tile]
                packets[r ^ r2, c ^ c2 ^ core] = value, jnp.broadcast_to(at, (slots, tile))

    def column_sums(core):
        sums = [jnp.zeros((slots, tile), jnp.float32)] * blocks
        for (_, c), (value, at) in packets.items():
            if c == core:
                sums = [s + jnp.where(at == p, value, 0.0) for p, s in enumerate(sums)]
        return sums

    def smooth_total(sums):
        total = jnp.zeros((slots, tile), jnp.float32)
        for s in sums:
            power = jnp.exp(0.75 * jnp.log(jnp.maximum(s, 1e-30)))
            total = total + jnp.where(s > 0.0, power, 0.0)
        return jnp.sum(total)

    sums = column_sums(0)
    first, second = smooth_total(sums), smooth_total(column_sums(1))
    total = first + second
    own = packets[0, 0][1]
    chosen = jnp.zeros((slots, tile), jnp.float32)
    for p in range(blocks):
        chosen = chosen + jnp.where(own == p, sums[p], 0.0)
    terms = jnp.where(own >= 0.0, -0.75 * jnp.log(jnp.maximum(chosen, 1e-30)), EMPTY)

    me = lax.axis_index("row")
    mine = lax.broadcasted_iota(jnp.int32, (slots, LANES), 0) == me
    position = {}
    for (r, c), (_, at) in packets.items():
        if c == 0:
            at = jnp.where(mine, at[:, :LANES], 0.0)
            position[r] = jnp.sum(at, axis=0, keepdims=True).astype(jnp.int32)
    for k, (a, b) in enumerate(order):
        at = position[a] if a == b else jnp.where(outer(me), position[a], position[b])
        incoming_ref[k : k + 1, :] = at

    both = mine_ref[:8, -tile:] + other_ref[:8, -tile:]
    shift = jnp.log(jnp.full((8, tile), total)) - jnp.log(both) - shift_log
    shift = jnp.transpose(shift)[:, :1]

    for s in range(slots):
        x = logs_ref[s] + shift + terms[s : s + 1]
        matrix_ref[s] = jnp.maximum(x, 0.0).astype(jnp.bfloat16)
    psi = psi_ref[...]
    for (a, b), out_ref in zip(order, out_refs, strict=True):
        s = jnp.bitwise_xor(me, a if a == b else jnp.where(outer(me), a, b))
        out_ref[...] = lax.dot_general(psi, matrix_ref[s], NN, preferred_element_type=jnp.float32)


def place(at_ref, refs, first, out_ref):
    tile = refs[0].shape[1]
    at = [jnp.max(at_ref[k : k + 1, :]) for k in first]
    for p, ref in zip(at, refs, strict=True):
        columns = pl.ds(pl.multiple_of(jnp.maximum(p, 0) * tile, tile), tile)
        out_ref[:, columns] += jnp.where(p >= 0, ref[...], 0.0)


def early_kernel(order, at_ref, matrix_ref, chosen_ref, *refs):
    *in_refs, range_ref, out_ref = refs
    out = jnp.zeros(range_ref.shape, jnp.float32)
    for s in range(matrix_ref.shape[0]):
        out = out + lax.dot_general(chosen_ref[s], matrix_ref[s], NT, preferred_element_type=jnp.float32)
    range_ref[...] = out
    out_ref[...] = jnp.zeros_like(out_ref)
    place(at_ref, in_refs, order, out_ref)


def late_kernel(order, at_ref, early_ref, mine_ref, other_ref, *refs):
    *in_refs, range_hbm, out_hbm, range_ref, out_ref, sems = refs
    out_ref[...] = early_ref[...]
    place(at_ref, in_refs, order, out_ref)
    range_ref[...] = mine_ref[...] + other_ref[...]
    rank = out_ref.shape[0]
    copies = [pltpu.make_async_copy(range_ref, range_hbm, sems.at[rank // 8])]
    for k in range(rank // 8):
        some = pl.ds(k * 8, 8)
        copies.append(pltpu.make_async_copy(out_ref.at[some], out_hbm.at[some], sems.at[k]))
    for copy in copies:
        copy.start()
    for copy in copies:
        copy.wait()


def on_device(counts, tile_pos, omega_t, psi):
    slots, tile, _ = counts.shape
    rank, width = omega_t.shape
    blocks = width // (slots * tile)
    rows = slots
    order = [(0, 0)] + rounds(rows)
    DMA = pltpu.SemaphoreType.DMA

    def call(kernel, name, outs, ins, out_specs=None, scratch=(), cost=None):
        return pl.pallas_call(
            kernel,
            out_shape=outs,
            in_specs=ins,
            out_specs=out_specs or (VMEM,) * len(outs),
            scratch_shapes=scratch,
            compiler_params=PARAMS,
            cost_estimate=cost,
            name=name,
        )

    def swap(x, far, near):
        return lax.ppermute(x, "row", [(i, i ^ (far if outer(i) else near)) for i in range(rows)])

    def across(x, k, odd):
        pairs = [(2 * i + c, 2 * (i ^ k) + (c ^ odd)) for i in range(rows) for c in range(2)]
        return lax.ppermute(x, ("row", "col"), pairs)

    def other_col(x):
        return lax.ppermute(x, "col", [(0, 1), (1, 0)])

    counts, tile_pos, omega_t, psi = (
        pltpu.with_memory_space_constraint(x, pltpu.HBM) for x in (counts, tile_pos, omega_t, psi)
    )
    packet, row_part, held = call(
        sums_kernel,
        "sums",
        (f32(slots, tile + LANES), f32(8, tile), bf16(slots, tile, tile)),
        [HBM, HBM],
        scratch=[pltpu.SMEM((slots,), jnp.int32), DMA(()), DMA((slots,))],
    )(tile_pos, counts)

    first, *later = stages(rows)
    packets = [packet] + [across(packet, k, odd) for k, odd in first]
    group = LANES // len(packets)
    lane = lax.broadcasted_iota(jnp.int32, (slots, LANES), 1)
    at = packet[:, tile:]
    for j, other in enumerate(packets):
        at = jnp.where(lane >= j * group, other[:, tile:], at)
    gathered = jnp.concatenate([x[:, :tile] for x in packets] + [at], axis=1)
    gathered, held = lax.optimization_barrier((gathered, held))
    near, far = [(0, 0)] + first, [(0, 0)]
    for ((k, odd),) in later:
        gathered = jnp.concatenate([gathered, across(gathered, k, odd)])
        far += [(r ^ k, c ^ odd) for r, c in far]
    logs, chosen, held_psi = call(
        lambda *refs: prepare_kernel(blocks, *refs),
        "prepare",
        (f32(slots, tile, tile), bf16(slots, rank, tile), bf16(*psi.shape)),
        [HBM, VMEM, HBM, HBM],
        scratch=[pltpu.SMEM((slots,), jnp.int32), DMA((slots + 2,))],
        cost=pl.CostEstimate(flops=40 * counts.size, bytes_accessed=6 * counts.size, transcendentals=counts.size),
    )(tile_pos, held, omega_t, psi)

    row_part = jnp.concatenate([row_part] * (gathered.shape[0] // row_part.shape[0]))
    gathered = jnp.concatenate([gathered, row_part], axis=1)
    gathered, logs, chosen, held_psi = lax.optimization_barrier((gathered, logs, chosen, held_psi))
    other = other_col(gathered)

    matrix, incoming_at, *parts = call(
        lambda *refs: matrix_kernel(blocks, near, far, order, *refs),
        "matrix",
        (bf16(*counts.shape), jax.ShapeDtypeStruct((rows, LANES), jnp.int32)) + (f32(rank, tile),) * rows,
        [VMEM] * 4,
    )(gathered, other, logs, held_psi)

    arrived = [swap(part, *ks) for part, ks in zip(parts[1:], order[1:], strict=True)]
    half = 2

    partial_range, early = call(
        lambda *refs: early_kernel(range(half + 1), *refs),
        "early",
        (f32(rank, tile), f32(rank, blocks * tile)),
        [VMEM] * (4 + half),
    )(incoming_at, matrix, chosen, parts[0], *arrived[:half])
    other_range = other_col(partial_range)
    return call(
        lambda *refs: late_kernel(range(half + 1, rows), *refs),
        "late",
        (f32(rank, tile), f32(rank, blocks * tile)),
        [VMEM] * (4 + rows - 1 - half),
        out_specs=(HBM, HBM),
        scratch=[pltpu.VMEM((rank, tile), jnp.float32), pltpu.VMEM((rank, blocks * tile), jnp.float32), DMA((rank // 8 + 1,))],
    )(incoming_at, early, partial_range, other_range, *arrived[half:])


def solution(mesh):
    placed = (
        P(("grp", "row", "col"), None, None),
        P(("grp", "row", "col")),
        P(None, "col"),
        P(None, "row"),
    )
    return jax.shard_map(
        on_device,
        mesh=mesh,
        in_specs=placed,
        out_specs=(P(None, ("grp", "row")), P(None, ("grp", "col", "row"))),
        check_vma=False,
    )
```

```python
import math

import jax
import jax.numpy as jnp
from jax import lax
from jax.experimental import pallas as pl
from jax.experimental.pallas import tpu as pltpu
from jax.sharding import PartitionSpec as P

shift_log = math.log(5.0)
LANES = 128
EMPTY = -1e30
PARAMS = pltpu.CompilerParams(vmem_limit_bytes=40 * 1024 * 1024)
VMEM = pl.BlockSpec(memory_space=pltpu.VMEM)
HBM = pl.BlockSpec(memory_space=pltpu.HBM)

NN = (((1,), (0,)), ((), ()))
NT = (((1,), (1,)), ((), ()))


def f32(*shape):
    return jax.ShapeDtypeStruct(shape, jnp.float32)


def bf16(*shape):
    return jax.ShapeDtypeStruct(shape, jnp.bfloat16)


def sums_kernel(pos_hbm, counts_hbm, packet_ref, row_ref, counts_ref, pos_ref, pos_sem, sems):
    slots, tile, _ = counts_ref.shape
    fetch_pos = pltpu.make_async_copy(pos_hbm, pos_ref, pos_sem)
    fetch_pos.start()
    fetches = [pltpu.make_async_copy(counts_hbm.at[s], counts_ref.at[s], sems.at[s]) for s in range(slots)]
    for fetch in fetches:
        fetch.start()
    fetch_pos.wait()

    values = jnp.zeros((tile, tile), jnp.float32)
    for g in range(0, slots, 8):
        columns = []
        for s in range(g, g + 8):
            fetches[s].wait()
            x = jnp.where(pos_ref[s] >= 0, counts_ref[s].astype(jnp.float32), 0.0)
            at = jnp.full((1, LANES), pos_ref[s].astype(jnp.float32))
            columns.append(jnp.concatenate([jnp.sum(x, axis=0, keepdims=True), at], axis=1))
            values = values + x
        packet_ref[g : g + 8, :] = jnp.concatenate(columns)
    narrow = sum(values[:, k : k + LANES] for k in range(0, tile, LANES))
    rows = jnp.sum(jnp.transpose(narrow), axis=0, keepdims=True)
    row_ref[...] = jnp.broadcast_to(rows, (8, tile))


def prepare_kernel(blocks, packet_ref, counts_ref, omega_hbm, psi_hbm, logs_ref, chosen_ref, psi_ref, sems):
    slots, tile, _ = counts_ref.shape
    fetches = [pltpu.make_async_copy(psi_hbm, psi_ref, sems.at[slots])]
    fetches[0].start()
    at = [jnp.max(packet_ref[s : s + 1, tile:]).astype(jnp.int32) for s in range(slots)]
    for s, p in enumerate(at):
        columns = pl.ds(pl.multiple_of((s * blocks + jnp.maximum(p, 0)) * tile, tile), tile)
        fetches.append(pltpu.make_async_copy(omega_hbm.at[:, columns], chosen_ref.at[s], sems.at[s]))
        fetches[-1].start()
    for s, p in enumerate(at):
        x = counts_ref[s].astype(jnp.float32)
        logs_ref[s] = jnp.log(jnp.where(p >= 0, x, 1.0))
    for fetch in fetches:
        fetch.wait()


def stages(rows):
    bits = [1 << k for k in range(2, rows.bit_length() - 1)]
    return [[(1, 1), (2, 1), (3, 0)]] + [[(bit, 1)] for bit in bits]


def partners(rows):
    if rows == 8:
        return [
            [4, 5, 6, 7, 0, 1, 2, 3],
            [6, 7, 3, 2, 5, 4, 0, 1],
            [7, 6, 5, 4, 3, 2, 1, 0],
            [3, 2, 1, 0, 7, 6, 5, 4],
            [5, 4, 7, 6, 1, 0, 3, 2],
            [2, 3, 0, 1, 6, 7, 4, 5],
            [1, 0, 4, 5, 2, 3, 7, 6],
        ]
    return [[row ^ k for row in range(rows)] for k in range(rows - 1, 0, -1)]


def pick(table, me):
    offsets = {row ^ other for row, other in enumerate(table)}
    if len(offsets) == 1:
        return jnp.bitwise_xor(me, offsets.pop())
    return sum(jnp.where(me == row, other, 0) for row, other in enumerate(table))


def matrix_kernel(blocks, near, far, order, mine_ref, other_ref, logs_ref, psi_ref, matrix_ref, incoming_ref, *out_refs):
    slots, tile, _ = logs_ref.shape
    rows = slots
    group = LANES // len(near)
    packets = {}
    for g, (r, c) in enumerate(far):
        some = slice(g * slots, (g + 1) * slots)
        for j, (r2, c2) in enumerate(near):
            for core, ref in enumerate((mine_ref, other_ref)):
                at = ref[some, len(near) * tile + j * group :][:, :1]
                value = ref[some, j * tile : (j + 1) * tile]
                packets[r ^ r2, c ^ c2 ^ core] = value, jnp.broadcast_to(at, (slots, tile))

    def column_sums(core):
        sums = [jnp.zeros((slots, tile), jnp.float32)] * blocks
        for (_, c), (value, at) in packets.items():
            if c == core:
                sums = [s + jnp.where(at == p, value, 0.0) for p, s in enumerate(sums)]
        return sums

    def smooth_total(sums):
        total = jnp.zeros((slots, tile), jnp.float32)
        for s in sums:
            power = jnp.exp(0.75 * jnp.log(jnp.maximum(s, 1e-30)))
            total = total + jnp.where(s > 0.0, power, 0.0)
        return jnp.sum(total)

    sums = column_sums(0)
    first, second = smooth_total(sums), smooth_total(column_sums(1))
    total = first + second
    own = packets[0, 0][1]
    chosen = jnp.zeros((slots, tile), jnp.float32)
    for p in range(blocks):
        chosen = chosen + jnp.where(own == p, sums[p], 0.0)
    terms = jnp.where(own >= 0.0, -0.75 * jnp.log(jnp.maximum(chosen, 1e-30)), EMPTY)

    me = lax.axis_index("row")
    mine = lax.broadcasted_iota(jnp.int32, (slots, LANES), 0) == me
    position = {}
    for (r, c), (_, at) in packets.items():
        if c == 0:
            at = jnp.where(mine, at[:, :LANES], 0.0)
            position[r] = jnp.sum(at, axis=0, keepdims=True).astype(jnp.int32)
    for r, at in position.items():
        incoming_ref[r : r + 1, :] = at

    both = mine_ref[:8, -tile:] + other_ref[:8, -tile:]
    shift = jnp.log(jnp.full((8, tile), total)) - jnp.log(both) - shift_log
    shift = jnp.transpose(shift)[:, :1]

    psi = psi_ref[...]
    row = lax.broadcasted_iota(jnp.int32, (slots, tile), 0)
    for table, out_ref in zip(order, out_refs, strict=True):
        s = pick(table, me)
        term = jnp.sum(jnp.where(row == s, terms, 0.0), axis=0, keepdims=True)
        x = jnp.maximum(logs_ref[s] + shift + term, 0.0).astype(jnp.bfloat16)
        matrix_ref[s] = x
        out_ref[...] = lax.dot_general(psi, x, NN, preferred_element_type=jnp.float32)


def place(at_ref, refs, tables, out_ref):
    tile = refs[0].shape[1]
    me = lax.axis_index("row")
    offset = lax.broadcasted_iota(jnp.int32, at_ref.shape, 0)
    at = [jnp.max(jnp.where(offset == jnp.bitwise_xor(me, pick(table, me)), at_ref[...], -1)) for table in tables]
    for p, ref in zip(at, refs, strict=True):
        columns = pl.ds(pl.multiple_of(jnp.maximum(p, 0) * tile, tile), tile)
        out_ref[:, columns] += jnp.where(p >= 0, ref[...], 0.0)


def early_kernel(order, at_ref, matrix_ref, chosen_ref, *refs):
    *in_refs, range_ref, out_ref = refs
    out = jnp.zeros(range_ref.shape, jnp.float32)
    for s in range(matrix_ref.shape[0]):
        out = out + lax.dot_general(chosen_ref[s], matrix_ref[s], NT, preferred_element_type=jnp.float32)
    range_ref[...] = out
    out_ref[...] = jnp.zeros_like(out_ref)
    place(at_ref, in_refs, order, out_ref)


def late_kernel(order, at_ref, early_ref, mine_ref, other_ref, *refs):
    *in_refs, range_hbm, out_hbm, range_ref, out_ref, sems = refs
    out_ref[...] = early_ref[...]
    place(at_ref, in_refs, order, out_ref)
    range_ref[...] = mine_ref[...] + other_ref[...]
    rank = out_ref.shape[0]
    copies = [pltpu.make_async_copy(range_ref, range_hbm, sems.at[rank // 8])]
    for k in range(rank // 8):
        some = pl.ds(k * 8, 8)
        copies.append(pltpu.make_async_copy(out_ref.at[some], out_hbm.at[some], sems.at[k]))
    for copy in copies:
        copy.start()
    for copy in copies:
        copy.wait()


def on_device(counts, tile_pos, omega_t, psi):
    slots, tile, _ = counts.shape
    rank, width = omega_t.shape
    blocks = width // (slots * tile)
    rows = slots
    order = [list(range(rows))] + partners(rows)
    DMA = pltpu.SemaphoreType.DMA

    def call(kernel, name, outs, ins, out_specs=None, scratch=(), cost=None):
        return pl.pallas_call(
            kernel,
            out_shape=outs,
            in_specs=ins,
            out_specs=out_specs or (VMEM,) * len(outs),
            scratch_shapes=scratch,
            compiler_params=PARAMS,
            cost_estimate=cost,
            name=name,
        )

    def swap(x, table):
        return lax.ppermute(x, "row", list(enumerate(table)))

    def across(x, k, odd):
        pairs = [(2 * i + c, 2 * (i ^ k) + (c ^ odd)) for i in range(rows) for c in range(2)]
        return lax.ppermute(x, ("row", "col"), pairs)

    def other_col(x):
        return lax.ppermute(x, "col", [(0, 1), (1, 0)])

    counts, tile_pos, omega_t, psi = (
        pltpu.with_memory_space_constraint(x, pltpu.HBM) for x in (counts, tile_pos, omega_t, psi)
    )
    packet, row_part, held = call(
        sums_kernel,
        "sums",
        (f32(slots, tile + LANES), f32(8, tile), bf16(slots, tile, tile)),
        [HBM, HBM],
        scratch=[pltpu.SMEM((slots,), jnp.int32), DMA(()), DMA((slots,))],
    )(tile_pos, counts)

    first, *later = stages(rows)
    packets = [packet] + [across(packet, k, odd) for k, odd in first]
    group = LANES // len(packets)
    lane = lax.broadcasted_iota(jnp.int32, (slots, LANES), 1)
    at = packet[:, tile:]
    for j, other in enumerate(packets):
        at = jnp.where(lane >= j * group, other[:, tile:], at)
    gathered = jnp.concatenate([x[:, :tile] for x in packets] + [at], axis=1)
    gathered, held = lax.optimization_barrier((gathered, held))
    near, far = [(0, 0)] + first, [(0, 0)]
    for ((k, odd),) in later:
        gathered = jnp.concatenate([gathered, across(gathered, k, odd)])
        far += [(r ^ k, c ^ odd) for r, c in far]
    logs, chosen, held_psi = call(
        lambda *refs: prepare_kernel(blocks, *refs),
        "prepare",
        (f32(slots, tile, tile), bf16(slots, rank, tile), bf16(*psi.shape)),
        [VMEM, VMEM, HBM, HBM],
        scratch=[DMA((slots + 1,))],
        cost=pl.CostEstimate(flops=40 * counts.size, bytes_accessed=6 * counts.size, transcendentals=counts.size),
    )(packet, held, omega_t, psi)

    row_part = jnp.concatenate([row_part] * (gathered.shape[0] // row_part.shape[0]))
    gathered = jnp.concatenate([gathered, row_part], axis=1)
    gathered, logs, chosen, held_psi = lax.optimization_barrier((gathered, logs, chosen, held_psi))
    other = other_col(gathered)

    matrix, incoming_at, *parts = call(
        lambda *refs: matrix_kernel(blocks, near, far, order, *refs),
        "matrix",
        (bf16(*counts.shape), jax.ShapeDtypeStruct((rows, LANES), jnp.int32)) + (f32(rank, tile),) * rows,
        [VMEM] * 4,
    )(gathered, other, logs, held_psi)

    arrived = [swap(part, table) for part, table in zip(parts[1:], order[1:], strict=True)]
    half = 3

    partial_range, early = call(
        lambda *refs: early_kernel(order[: half + 1], *refs),
        "early",
        (f32(rank, tile), f32(rank, blocks * tile)),
        [VMEM] * (4 + half),
    )(incoming_at, matrix, chosen, parts[0], *arrived[:half])
    other_range = other_col(partial_range)
    return call(
        lambda *refs: late_kernel(order[half + 1 :], *refs),
        "late",
        (f32(rank, tile), f32(rank, blocks * tile)),
        [VMEM] * (4 + rows - 1 - half),
        out_specs=(HBM, HBM),
        scratch=[pltpu.VMEM((rank, tile), jnp.float32), pltpu.VMEM((rank, blocks * tile), jnp.float32), DMA((rank // 8 + 1,))],
    )(incoming_at, early, partial_range, other_range, *arrived[half:])


def solution(mesh):
    placed = (
        P(("grp", "row", "col"), None, None),
        P(("grp", "row", "col")),
        P(None, "col"),
        P(None, "row"),
    )
    return jax.shard_map(
        on_device,
        mesh=mesh,
        in_specs=placed,
        out_specs=(P(None, ("grp", "row")), P(None, ("grp", "col", "row"))),
        check_vma=False,
    )
```
